32 devices in a mesh: row: 8 (over y, x, core), col: 4 (over z).
Axes of the slice: x: 2, y: 2, z: 4, core: 2. Of those that a mesh axis runs over, the one named last changes fastest.
Arguments:
- queries: bfloat16 [128, 16, 1024], P('row', None, 'col'), may hold values from -30 to 30
- new_keys: bfloat16 [128, 1024], P('row', 'col'), may hold values from -6 to 6
- new_values: bfloat16 [128, 1024], P('row', 'col'), may hold values from -12 to 12
- cache_keys: bfloat16 [128, 128, 1024], P('row', None, 'col'), may hold values from -8 to 8
- cache_values: bfloat16 [128, 128, 1024], P('row', None, 'col'), may hold values from -12 to 12
- lengths: int32 [128], P('row'), may hold values from 64 to 128
- parents: int32 [128], P('row'), may hold values from 0 to 127, as said below
- residual: bfloat16 [128, 16, 1024], P('row', None, 'col'), may hold values from -20 to 20
- norm_gain: bfloat16 [16, 1024], P(None, 'col'), may hold values from 0.5 to 1.5
- vocab_weight: bfloat16 [16, 1024, 64128], P(None, 'col', 'row')
Outputs:
- logprobs: float32 [128, 64128], P('col', 'row')
The draws below stay inside these ranges and needn't reach their ends.
Inputs may be any that keep to these rules, and one draw needn't show every extreme that they name: Among the 16 child beams of one index of row, at most 4 have their parents on the beams of any single index of row, and exactly 4 do for some index.
All inputs are finite; a program needn't handle non-finite values.
Results may differ from the reference program's by a relative error of at most 0.0015.
Values may be sent and summed in bfloat16 or wider, within the bound.
A program may use at most 128 MiB of HBM per device.

```python
import jax
import jax.numpy as jnp
from jax import lax

KV_HEADS = 8
HEAD_DIM = 128
GROUP = 16
D = 16384
VOCAB = 64128
BEAMS_DEV = 16
BEAMS = 128
CTX = 128
CAP = 4
N_ROW = 8


def draw_queries(key, part):
    key_a = jax.random.fold_in(jax.random.fold_in(key, 11), 0)
    kv_width = KV_HEADS * HEAD_DIM
    noise_part = jax.random.normal(key_a, (BEAMS, GROUP, kv_width), jnp.float32)
    return jnp.clip(noise_part, -6.0, 6.0).astype(jnp.bfloat16)


def draw_cache_keys(key, part):
    kv_width = KV_HEADS * HEAD_DIM
    noise_part = jnp.clip(jax.random.normal(jax.random.fold_in(key, 13), (BEAMS, CTX, kv_width), jnp.float32), -6.0, 6.0)
    return noise_part.astype(jnp.bfloat16)


def draw_residual(key, part):
    key_a, key_b, key_c = jax.random.split(jax.random.fold_in(key, 17), 3)
    kv_width = KV_HEADS * HEAD_DIM
    row_scale = 10.0 ** jax.random.uniform(key_a, (BEAMS, 1, 1), jnp.float32)
    rising = 0.5 * jnp.arange(kv_width, dtype=jnp.float32) / kv_width
    col_scale = 10.0 ** (rising[None, None, :] + 0.5 * jax.random.uniform(key_b, (1, GROUP, kv_width), jnp.float32))
    base_part = jnp.clip(jax.random.normal(key_c, (BEAMS, GROUP, kv_width), jnp.float32), -4.0, 4.0)
    return (0.05 * row_scale * col_scale * base_part).astype(jnp.bfloat16)


def draw_vocab_weight(key, part):
    kv_width = KV_HEADS * HEAD_DIM
    shape_full = (GROUP, kv_width, VOCAB)
    factor = 3.0 / D ** 0.5 * (0.9 + 0.25 * jnp.arange(VOCAB, dtype=jnp.float32) / VOCAB)
    key_a = jax.random.fold_in(key, 19)
    base_part = jnp.clip(jax.random.normal(key_a, shape_full, jnp.float32), -6.0, 6.0)
    return (base_part * factor[None, None, :]).astype(jnp.bfloat16)


def draw_parents(key, part):
    base_key = jax.random.fold_in(key, 23)
    pool_size = CAP * N_ROW

    def per_device(device_index):
        sub_key = jax.random.fold_in(base_key, device_index)
        key_a, key_b, key_c, key_d = jax.random.split(sub_key, 4)
        owners = jnp.arange(pool_size, dtype=jnp.int32) // CAP
        favour = jax.random.randint(key_a, (), 0, N_ROW)
        draw_ranks = jax.random.permutation(key_b, pool_size).astype(jnp.int32)
        draw_ranks = jnp.where(owners == favour, -1 - jnp.arange(pool_size, dtype=jnp.int32) % CAP, draw_ranks)
        chosen = jnp.argsort(draw_ranks, stable=True)[:BEAMS_DEV]
        shuffle = jax.random.permutation(key_c, BEAMS_DEV)
        sources = owners[chosen][shuffle]
        offsets = jax.random.randint(key_d, (BEAMS_DEV,), 0, BEAMS_DEV)
        return (sources * BEAMS_DEV + offsets).astype(jnp.int32)
    return jax.vmap(per_device)(jnp.arange(N_ROW, dtype=jnp.int32)).reshape(BEAMS).astype(jnp.int32)


def plant(result, key, low, high):
    index_at = [jax.random.randint(jax.random.fold_in(key, axis), (), 0, length) for axis, length in enumerate(result.shape)]
    longest = result.shape.index(max(result.shape))
    neighbour = index_at[:longest] + [(index_at[longest] + 1) % result.shape[longest]] + index_at[longest + 1:]
    return result.at[tuple(index_at)].set(low).at[tuple(neighbour)].set(high)


def shard_levels(key, dims, pieces, low, high):
    loudness, own = 1.0, jax.random.fold_in(key, 6)
    for axis_at, blocks in pieces:
        steps = jnp.exp(jax.random.uniform(jax.random.fold_in(own, axis_at), (blocks,), jnp.float32, low / len(pieces), high / len(pieces)))
        loudness = loudness * jnp.repeat(steps, dims[axis_at] // blocks).reshape([-1 if axis == axis_at else 1 for axis in range(len(dims))])
    return loudness


def bell_draw(own_key, dims, scale, most, cuts=(), held_as=jnp.bfloat16):
    values = jax.random.normal(own_key, dims, jnp.float32) * scale
    if len(cuts) > 0:
        values = shard_levels(own_key, dims, cuts, -0.22, 0.18) * values
    return jnp.clip(values, min=-most, max=most).astype(held_as)


def setup_inputs(seed: int = 0) -> dict:
    arg_keys = jax.random.split(jax.random.key(seed), 11)
    return {
        "queries": draw_queries(jax.random.fold_in(arg_keys[10], 71), 0),
        "new_keys": bell_draw(arg_keys[1], (BEAMS, KV_HEADS * HEAD_DIM), 1.0, 6.0, ((0, 8), (1, 4))),
        "new_values": bell_draw(arg_keys[2], (BEAMS, KV_HEADS * HEAD_DIM), 2.0, 12.0, ((0, 8), (1, 4))),
        "cache_keys": draw_cache_keys(jax.random.fold_in(arg_keys[10], 71), 0),
        "cache_values": bell_draw(arg_keys[4], (BEAMS, CTX, KV_HEADS * HEAD_DIM), 2.0, 12.0, ((0, 8), (2, 4))),
        "lengths": plant(jax.random.randint(arg_keys[5], (BEAMS,), CTX // 2, CTX + 1), jax.random.fold_in(arg_keys[5], 1), CTX // 2, CTX).astype(jnp.int32),
        "parents": draw_parents(jax.random.fold_in(arg_keys[10], 71), 0),
        "residual": draw_residual(jax.random.fold_in(arg_keys[10], 71), 0),
        "norm_gain": jnp.clip(1.0 + 0.1 * jax.random.normal(arg_keys[8], (GROUP, KV_HEADS * HEAD_DIM), jnp.float32), 0.5, 1.5).astype(jnp.bfloat16),
        "vocab_weight": draw_vocab_weight(jax.random.fold_in(arg_keys[10], 71), 0),
    }


def reference(queries, new_keys, new_values, cache_keys, cache_values, lengths, parents, residual, norm_gain, vocab_weight):
    scale_factor = HEAD_DIM ** (-0.5)
    kept_keys = jnp.take(cache_keys, parents, axis=0)
    kept_values = jnp.take(cache_values, parents, axis=0)
    live_rows = jnp.take(lengths, parents, axis=0)
    query_heads = queries.astype(jnp.float32).reshape(BEAMS, GROUP, KV_HEADS, HEAD_DIM)
    key_heads = kept_keys.astype(jnp.float32).reshape(BEAMS, CTX, KV_HEADS, HEAD_DIM)
    value_heads = kept_values.astype(jnp.float32).reshape(BEAMS, CTX, KV_HEADS, HEAD_DIM)
    fresh_keys = new_keys.astype(jnp.float32).reshape(BEAMS, KV_HEADS, HEAD_DIM)
    fresh_values = new_values.astype(jnp.float32).reshape(BEAMS, 1, KV_HEADS, HEAD_DIM)
    cached = jnp.einsum('bjge,btge->bjgt', query_heads, key_heads, precision=lax.Precision.HIGHEST) * scale_factor
    own_score = jnp.einsum('bjge,bge->bjg', query_heads, fresh_keys, precision=lax.Precision.HIGHEST) * scale_factor
    positions = jnp.arange(CTX, dtype=jnp.int32)[None, None, None, :]
    visible = positions < live_rows[:, None, None, None]
    peak_score = jnp.maximum(lax.optimization_barrier(jnp.max(jnp.where(visible, cached, -jnp.inf), axis=-1)), own_score)
    weight = jnp.where(visible, jnp.exp(cached - peak_score[..., None]), jnp.float32(0.0))
    weight_own = jnp.exp(own_score - peak_score)
    weight_sum = lax.optimization_barrier(jnp.sum(weight, axis=-1)) + weight_own
    rounded = lax.optimization_barrier(weight.astype(jnp.bfloat16)).astype(jnp.float32)
    rounded_own = lax.optimization_barrier(weight_own.astype(jnp.bfloat16)).astype(jnp.float32)
    summed = jnp.einsum('bjgt,btge->bjge', rounded, value_heads, precision=lax.Precision.HIGHEST)
    own_part = rounded_own[..., None] * fresh_values
    attended = ((summed + own_part) / weight_sum[..., None]).reshape(BEAMS, GROUP, KV_HEADS * HEAD_DIM).astype(jnp.bfloat16)
    stream = residual.astype(jnp.float32) + attended.astype(jnp.float32)
    scaling = lax.rsqrt(lax.optimization_barrier(jnp.sum(stream * stream, axis=(1, 2))) / D + 1e-05)
    normed = (stream * norm_gain.astype(jnp.float32)[None] * scaling[:, None, None]).astype(jnp.bfloat16)
    logits = jnp.dot(normed.reshape(BEAMS, D), vocab_weight.reshape(D, VOCAB), preferred_element_type=jnp.float32)
    totals = lax.optimization_barrier(jnp.sum(jnp.exp(logits), axis=1))
    return logits - jnp.log(totals)[:, None]
```

```python
import jax
import jax.numpy as jnp
from jax import lax
from jax.sharding import PartitionSpec as P

HEAD_DIM = 128
D = 16384


def from_partner(value, axis, distance):
    mask = 2**distance
    pairs = [(source, source ^ mask) for source in range(lax.axis_size(axis))]
    return lax.ppermute(value, axis, pairs)


def count_before(sources):
    entries = sources.shape[-1]
    earlier = jnp.arange(entries)[:, None] > jnp.arange(entries)[None, :]
    matching = sources[..., :, None] == sources[..., None, :]
    return jnp.sum(matching & earlier, axis=-1)


def attend(queries_in, key_cache, value_cache, key_new, value_new, live_rows):
    leading = queries_in.shape[:-2]
    group_size = queries_in.shape[-2]
    panel_width = queries_in.shape[-1]
    head_part = min(panel_width, HEAD_DIM)
    heads_here = panel_width // head_part
    context = key_cache.shape[-2]
    query_heads = queries_in.reshape(leading + (group_size, heads_here, head_part))
    key_heads = key_cache.reshape(leading + (context, heads_here, head_part))
    value_heads = value_cache.reshape(leading + (context, heads_here, head_part))
    fresh_key = key_new.reshape(leading + (heads_here, head_part))
    fresh_value = value_new.reshape(leading + (1, heads_here, head_part)).astype(jnp.float32)
    cached = jnp.einsum(
        "...jhe,...the->...jht", query_heads, key_heads, preferred_element_type=jnp.float32
    )
    own_score = jnp.einsum(
        "...jhe,...he->...jh", query_heads, fresh_key, preferred_element_type=jnp.float32
    )
    partners = (HEAD_DIM // head_part).bit_length() - 1
    for bit_index in range(partners):
        other_cached, other_own = from_partner((cached, own_score), "col", bit_index)
        cached = cached + other_cached
        own_score = own_score + other_own
    scale_factor = HEAD_DIM ** (-0.5)
    cached = cached * scale_factor
    own_score = own_score * scale_factor
    positions = lax.broadcasted_iota(jnp.int32, cached.shape, cached.ndim - 1)
    visible = positions < live_rows.reshape(leading + (1, 1, 1))
    peak_score = jnp.maximum(jnp.max(jnp.where(visible, cached, -jnp.inf), axis=-1), own_score)
    weight = jnp.where(visible, jnp.exp(cached - peak_score[..., None]), jnp.float32(0.0))
    weight_own = jnp.exp(own_score - peak_score)
    weight_sum = jnp.sum(weight, axis=-1) + weight_own
    rounded = weight.astype(jnp.bfloat16)
    rounded_own = lax.optimization_barrier(weight_own.astype(jnp.bfloat16)).astype(jnp.float32)
    summed = jnp.einsum(
        "...jht,...the->...jhe", rounded, value_heads, preferred_element_type=jnp.float32
    )
    own_part = rounded_own[..., None] * fresh_value
    result = (summed + own_part) / weight_sum[..., None]
    return result.reshape(leading + (group_size, panel_width)).astype(jnp.bfloat16)


def body(
    queries,
    new_keys,
    new_values,
    cache_keys,
    cache_values,
    lengths,
    parents,
    residual,
    norm_gain,
    vocab_weight,
):
    row_count = lax.axis_size("row")
    beam_count = parents.shape[0]
    slot_cap = max(2, (2 * beam_count + row_count - 1) // row_count)
    group_size = queries.shape[1]
    panel_width = queries.shape[2]
    source = parents // beam_count
    slot_index = source * slot_cap + count_before(source)
    slots = row_count * slot_cap
    taken = slot_index[None, :] == jnp.arange(slots, dtype=jnp.int32)[:, None]
    child_of = jnp.sum(jnp.where(taken, jnp.arange(beam_count, dtype=jnp.int32)[None], 0), axis=1)
    offset = (parents % beam_count).astype(jnp.bfloat16)
    offset_row = jnp.broadcast_to(offset[:, None, None], (beam_count, 1, panel_width))
    request = jnp.concatenate(
        [queries, new_keys[:, None], new_values[:, None], offset_row], axis=1
    )[child_of]
    asked = lax.all_to_all(request, "row", split_axis=0, concat_axis=0, tiled=True)
    wanted = asked[:, group_size + 2, 0].astype(jnp.int32)
    answer = attend(
        asked[:, :group_size],
        cache_keys[wanted],
        cache_values[wanted],
        asked[:, group_size],
        asked[:, group_size + 1],
        lengths[wanted],
    )
    attended = lax.all_to_all(answer, "row", split_axis=0, concat_axis=0, tiled=True)[slot_index]
    stream = residual.astype(jnp.float32) + attended.astype(jnp.float32)
    square_sums = lax.psum(jnp.sum(stream * stream, axis=(1, 2)), "col")
    scaling = lax.rsqrt(square_sums / D + 1e-05)
    normed = (stream * norm_gain.astype(jnp.float32)[None] * scaling[:, None, None]).astype(
        jnp.bfloat16
    )
    gathered = lax.all_gather(normed, "row", axis=0, tiled=True)
    flat_rows = gathered.reshape(gathered.shape[0], group_size * panel_width)
    flat_weight = vocab_weight.reshape(group_size * panel_width, vocab_weight.shape[2])
    partial = jnp.dot(flat_rows, flat_weight, preferred_element_type=jnp.float32)
    logits = lax.psum_scatter(
        partial.astype(jnp.bfloat16), "col", scatter_dimension=0, tiled=True
    ).astype(jnp.float32)
    totals = lax.psum(jnp.sum(jnp.exp(logits), axis=1), "row")
    return logits - jnp.log(totals)[:, None]


def solution(mesh):
    placed = (
        P("row", None, "col"),
        P("row", "col"),
        P("row", "col"),
        P("row", None, "col"),
        P("row", None, "col"),
        P("row"),
        P("row"),
        P("row", None, "col"),
        P(None, "col"),
        P(None, "col", "row"),
    )
    return jax.shard_map(
        body, mesh=mesh, in_specs=placed, out_specs=P("col", "row"), check_vma=False
    )
```

```python
import functools

import jax
import jax.numpy as jnp
from jax import lax
from jax.experimental import pallas as pl
from jax.experimental.pallas import tpu as pltpu
from jax.sharding import PartitionSpec as P

HEAD_DIM = 128
D = 16384
MESH = pl.DeviceIdType.MESH
LANES = 128
CHUNK = 512
PIECE = 256
SLOTS = 10


def from_partner(value, axis, distance):
    mask = 2**distance
    pairs = [(source, source ^ mask) for source in range(lax.axis_size(axis))]
    return lax.ppermute(value, axis, pairs)


def count_before(sources):
    entries = sources.shape[-1]
    earlier = jnp.arange(entries)[:, None] > jnp.arange(entries)[None, :]
    matching = sources[..., :, None] == sources[..., None, :]
    return jnp.sum(matching & earlier, axis=-1)


def attend(queries_in, key_cache, value_cache, key_new, value_new, live_rows):
    leading = queries_in.shape[:-2]
    group_size = queries_in.shape[-2]
    panel_width = queries_in.shape[-1]
    head_part = min(panel_width, HEAD_DIM)
    heads_here = panel_width // head_part
    context = key_cache.shape[-2]
    query_heads = queries_in.reshape(leading + (group_size, heads_here, head_part))
    key_heads = key_cache.reshape(leading + (context, heads_here, head_part))
    value_heads = value_cache.reshape(leading + (context, heads_here, head_part))
    fresh_key = key_new.reshape(leading + (heads_here, head_part))
    fresh_value = value_new.reshape(leading + (1, heads_here, head_part)).astype(jnp.float32)
    cached = jnp.einsum(
        "...jhe,...the->...jht", query_heads, key_heads, preferred_element_type=jnp.float32
    )
    own_score = jnp.einsum(
        "...jhe,...he->...jh", query_heads, fresh_key, preferred_element_type=jnp.float32
    )
    partners = (HEAD_DIM // head_part).bit_length() - 1
    for bit_index in range(partners):
        other_cached, other_own = from_partner((cached, own_score), "col", bit_index)
        cached = cached + other_cached
        own_score = own_score + other_own
    scale_factor = HEAD_DIM ** (-0.5)
    cached = cached * scale_factor
    own_score = own_score * scale_factor
    positions = lax.broadcasted_iota(jnp.int32, cached.shape, cached.ndim - 1)
    visible = positions < live_rows.reshape(leading + (1, 1, 1))
    peak_score = jnp.maximum(jnp.max(jnp.where(visible, cached, -jnp.inf), axis=-1), own_score)
    weight = jnp.where(visible, jnp.exp(cached - peak_score[..., None]), jnp.float32(0.0))
    weight_own = jnp.exp(own_score - peak_score)
    weight_sum = jnp.sum(weight, axis=-1) + weight_own
    rounded = weight.astype(jnp.bfloat16)
    rounded_own = lax.optimization_barrier(weight_own.astype(jnp.bfloat16)).astype(jnp.float32)
    summed = jnp.einsum(
        "...jht,...the->...jhe", rounded, value_heads, preferred_element_type=jnp.float32
    )
    own_part = rounded_own[..., None] * fresh_value
    result = (summed + own_part) / weight_sum[..., None]
    return result.reshape(leading + (group_size, panel_width)).astype(jnp.bfloat16)


def project_kernel(
    n_row,
    n_col,
    x_ref,
    square_ref,
    weight_ref,
    out_ref,
    rows,
    squares,
    squares_in,
    weights,
    weights_last,
    own,
    outgoing,
    incoming,
    total_out,
    total_in,
    weight_sem,
    last_sem,
    gather_send,
    gather_recv,
    gather_sq_send,
    gather_sq_recv,
    square_send,
    square_recv,
    part_send,
    part_recv,
    total_send,
    total_recv,
):
    row, col = lax.axis_index("row"), lax.axis_index("col")
    beams = x_ref.shape[0]
    groups, vocab, panel = weight_ref.shape
    owned = out_ref.shape[0]
    full = vocab // CHUNK
    last = vocab - full * CHUNK
    last_pad = own.shape[1] - full * CHUNK
    slots = weights.shape[0]
    chips = n_row // 2
    core = lax.rem(row, 2)
    chip = lax.div(row, 2)

    def fetch(chunk, slot):
        return pltpu.make_async_copy(
            weight_ref.at[:, pl.ds(pl.multiple_of(chunk * CHUNK, CHUNK), CHUNK), :],
            weights.at[slot],
            weight_sem.at[slot],
        )

    def fetch_last():
        return pltpu.make_async_copy(
            weight_ref.at[:, pl.ds(full * CHUNK, last), :], weights_last, last_sem.at[0]
        )

    if last:
        fetch_last().start()
    for slot in range(min(slots, full)):
        fetch(slot, slot).start()

    barrier = pltpu.get_barrier_semaphore()
    for k in range(1, n_row):
        pl.semaphore_signal(
            barrier, inc=1, device_id=(lax.rem(row + k, n_row), col), device_id_type=MESH
        )
    for k in range(1, n_col):
        pl.semaphore_signal(
            barrier, inc=1, device_id=(row, lax.rem(col + k, n_col)), device_id_type=MESH
        )
    pl.semaphore_wait(barrier, n_row - 1 + n_col - 1)

    def place(of_row):
        first = of_row * beams
        block = lax.rem(lax.div(first, owned) - col + n_col, n_col)
        return pl.ds(pl.multiple_of(block * owned + lax.rem(first, owned), beams), beams)

    def share(source, target, of_row, to_row, send, recv, index):
        return pltpu.make_async_remote_copy(
            src_ref=source,
            dst_ref=target.at[place(of_row)],
            send_sem=send.at[index],
            recv_sem=recv.at[index],
            device_id=(to_row, col),
            device_id_type=MESH,
        )

    mate = chip * 2 + 1 - core
    started = []
    for k in list(range(1, chips)) + [0]:
        to_row = lax.rem(chip + k, chips) * 2 + core if k else mate
        one = share(x_ref, rows, row, to_row, gather_send, gather_recv, k)
        two = share(square_ref, squares, row, to_row, gather_sq_send, gather_sq_recv, k)
        one.start()
        two.start()
        started += [one, two]
    rows[place(row)] = x_ref[...]
    squares[place(row)] = square_ref[...]
    pad = own.shape[1] - full * CHUNK
    if pad > last:
        edge = own.shape[1] - LANES
        outgoing[:, :, edge:] = jnp.zeros(outgoing.shape[:2] + (LANES,), outgoing.dtype)
        own[:, edge:] = jnp.zeros((owned, LANES), own.dtype)
    forwarded = []
    for k in range(1, chips):
        from_row = lax.rem(chip - k + chips, chips) * 2 + core
        share(rows.at[place(from_row)], rows, row, mate, gather_send, gather_recv, k).wait_recv()
        share(
            squares.at[place(from_row)], squares, row, mate, gather_sq_send, gather_sq_recv, k
        ).wait_recv()
        one = share(
            rows.at[place(from_row)], rows, from_row, mate, gather_send, gather_recv, chips + k
        )
        two = share(
            squares.at[place(from_row)],
            squares,
            from_row,
            mate,
            gather_sq_send,
            gather_sq_recv,
            chips + k,
        )
        one.start()
        two.start()
        forwarded += [one, two]
    for copy in started[-2:]:
        copy.wait_recv()
    for copy in forwarded:
        copy.wait_recv()

    square_copies = []
    for j in range(1, n_col):
        copy = pltpu.make_async_remote_copy(
            src_ref=squares.at[pl.ds(j * owned, owned)],
            dst_ref=squares_in.at[j - 1],
            send_sem=square_send.at[j - 1],
            recv_sem=square_recv.at[j - 1],
            device_id=(row, lax.rem(col + j, n_col)),
            device_id_type=MESH,
        )
        copy.start()
        square_copies.append(copy)

    def part_copy(j, chunk, columns):
        return pltpu.make_async_remote_copy(
            src_ref=outgoing.at[j - 1, :, columns],
            dst_ref=incoming.at[j - 1, :, columns],
            send_sem=part_send.at[chunk, j - 1],
            recv_sem=part_recv.at[chunk, j - 1],
            device_id=(row, lax.rem(col + j, n_col)),
            device_id_type=MESH,
        )

    def columns_of(chunk):
        return pl.ds(pl.multiple_of(chunk * CHUNK, CHUNK), CHUNK)

    last_columns = pl.ds(full * CHUNK, last_pad)

    def product(block, first, width):
        part = jnp.zeros((rows.shape[0], width), jnp.float32)
        for group in range(groups):
            part = part + lax.dot_general(
                rows[:, group * panel : (group + 1) * panel],
                block[group, first : first + width],
                (((1,), (1,)), ((), ())),
                preferred_element_type=jnp.float32,
            )
        return part

    def keep(part, columns):
        own[:, columns] = part[:owned]
        for j in range(1, n_col):
            outgoing[j - 1, :, columns] = part[j * owned : (j + 1) * owned].astype(jnp.bfloat16)

    if last:
        fetch_last().wait()
        for first in range(0, last, PIECE):
            width = min(PIECE, last - first)
            keep(
                product(weights_last, first, width),
                slice(full * CHUNK + first, full * CHUNK + first + width),
            )
        for j in range(1, n_col):
            part_copy(j, full, last_columns).start()

    def multiply(chunk, carry):
        slot = lax.rem(chunk, slots)
        fetch(chunk, slot).wait()
        for first in range(0, CHUNK, PIECE):
            columns = pl.ds(pl.multiple_of(chunk * CHUNK + first, PIECE), PIECE)
            keep(product(weights.at[slot], first, PIECE), columns)
        for j in range(1, n_col):
            part_copy(j, chunk, columns_of(chunk)).start()

        @pl.when(chunk + slots < full)
        def _():
            fetch(chunk + slots, slot).start()

        return carry

    lax.fori_loop(0, full, multiply, 0)

    square_sum = squares[:owned]
    for j in range(1, n_col):
        square_copies[j - 1].wait_recv()
        square_sum = square_sum + squares_in[j - 1]
    scale = lax.rsqrt(square_sum / D + 1e-05)[:, :1]

    def combine(chunk, columns):
        logits = own[:, columns]
        for j in range(1, n_col):
            part_copy(j, chunk, columns).wait_recv()
            logits = logits + incoming[j - 1, :, columns].astype(jnp.float32)
        logits = logits * scale
        own[:, columns] = logits
        return logits

    sums = jnp.zeros((owned, 1), jnp.float32)
    if last:
        logits = combine(full, last_columns)
        sums = sums + jnp.sum(jnp.exp(logits[:, :last]), axis=1, keepdims=True)

    def finish(chunk, sums):
        logits = combine(chunk, columns_of(chunk))
        return sums + jnp.sum(jnp.exp(logits), axis=1, keepdims=True)

    sums = lax.fori_loop(0, full, finish, sums)
    total_out[...] = jnp.broadcast_to(sums, total_out.shape)
    total_copies = []
    for k in range(1, n_row):
        copy = pltpu.make_async_remote_copy(
            src_ref=total_out,
            dst_ref=total_in.at[k - 1],
            send_sem=total_send.at[k - 1],
            recv_sem=total_recv.at[k - 1],
            device_id=(lax.rem(row + k, n_row), col),
            device_id_type=MESH,
        )
        copy.start()
        total_copies.append(copy)
    for copy in started + forwarded + square_copies:
        copy.wait_send()

    def sent(chunk, carry):
        for j in range(1, n_col):
            part_copy(j, chunk, columns_of(chunk)).wait_send()
        return carry

    lax.fori_loop(0, full, sent, 0)
    if last:
        for j in range(1, n_col):
            part_copy(j, full, last_columns).wait_send()
    total = total_out[...]
    for copy in total_copies:
        copy.wait_recv()
    for k in range(1, n_row):
        total = total + total_in[k - 1]
    out_ref[...] = own[:, :vocab] - jnp.log(total)[:, :1]
    for copy in total_copies:
        copy.wait_send()


def project(x, square_sums, weight):
    n_row, n_col = lax.axis_size("row"), lax.axis_size("col")
    beams, depth = x.shape
    groups, vocab, panel = weight.shape
    everyone = beams * n_row
    owned = everyone // n_col
    full = vocab // CHUNK
    last = vocab - full * CHUNK
    wide = full * CHUNK + -(-last // LANES) * LANES
    slots = min(SLOTS, full)
    chips = n_row // 2
    others = n_col - 1
    dma = pltpu.SemaphoreType.DMA
    vmem = pl.BlockSpec(memory_space=pltpu.VMEM)
    return pl.pallas_call(
        functools.partial(project_kernel, n_row, n_col),
        out_shape=jax.ShapeDtypeStruct((owned, vocab), jnp.float32),
        in_specs=[vmem, vmem, pl.BlockSpec(memory_space=pl.ANY)],
        out_specs=vmem,
        scratch_shapes=[
            pltpu.VMEM((everyone, depth), jnp.bfloat16),
            pltpu.VMEM((everyone, LANES), jnp.float32),
            pltpu.VMEM((others, owned, LANES), jnp.float32),
            pltpu.VMEM((slots, groups, CHUNK, panel), jnp.bfloat16),
            pltpu.VMEM((groups, max(last, 16), panel), jnp.bfloat16),
            pltpu.VMEM((owned, wide), jnp.float32),
            pltpu.VMEM((others, owned, wide), jnp.bfloat16),
            pltpu.VMEM((others, owned, wide), jnp.bfloat16),
            pltpu.VMEM((owned, LANES), jnp.float32),
            pltpu.VMEM((n_row - 1, owned, LANES), jnp.float32),
            dma((slots,)),
            dma((1,)),
            dma((2 * chips,)),
            dma((2 * chips,)),
            dma((2 * chips,)),
            dma((2 * chips,)),
            dma((others,)),
            dma((others,)),
            dma((full + 1, others)),
            dma((full + 1, others)),
            dma((n_row - 1,)),
            dma((n_row - 1,)),
        ],
        compiler_params=pltpu.CompilerParams(
            collective_id=0, has_side_effects=True, vmem_limit_bytes=56 * 2**20
        ),
        cost_estimate=pl.CostEstimate(
            flops=2 * everyone * depth * vocab,
            bytes_accessed=2 * depth * vocab,
            transcendentals=owned * vocab,
        ),
    )(x, square_sums, weight)


def project_whole(stream, norm_gain, vocab_weight):
    group_size, panel_width = norm_gain.shape
    square_sums = lax.psum(jnp.sum(stream * stream, axis=(1, 2)), "col")
    scaling = lax.rsqrt(square_sums / D + 1e-05)
    normed = (stream * norm_gain.astype(jnp.float32)[None] * scaling[:, None, None]).astype(
        jnp.bfloat16
    )
    gathered = lax.all_gather(normed, "row", axis=0, tiled=True)
    flat_rows = gathered.reshape(gathered.shape[0], group_size * panel_width)
    flat_weight = vocab_weight.reshape(group_size * panel_width, vocab_weight.shape[2])
    partial = jnp.dot(flat_rows, flat_weight, preferred_element_type=jnp.float32)
    logits = lax.psum_scatter(
        partial.astype(jnp.bfloat16), "col", scatter_dimension=0, tiled=True
    ).astype(jnp.float32)
    totals = lax.psum(jnp.sum(jnp.exp(logits), axis=1), "row")
    return logits - jnp.log(totals)[:, None]


def body(
    queries,
    new_keys,
    new_values,
    cache_keys,
    cache_values,
    lengths,
    parents,
    residual,
    norm_gain,
    vocab_weight,
):
    row_count = lax.axis_size("row")
    beam_count = parents.shape[0]
    slot_cap = max(2, (2 * beam_count + row_count - 1) // row_count)
    group_size = queries.shape[1]
    panel_width = queries.shape[2]
    source = parents // beam_count
    slot_index = source * slot_cap + count_before(source)
    slots = row_count * slot_cap
    taken = slot_index[None, :] == jnp.arange(slots, dtype=jnp.int32)[:, None]
    child_of = jnp.sum(jnp.where(taken, jnp.arange(beam_count, dtype=jnp.int32)[None], 0), axis=1)
    offset = (parents % beam_count).astype(jnp.bfloat16)
    offset_row = jnp.broadcast_to(offset[:, None, None], (beam_count, 1, panel_width))
    request = jnp.concatenate(
        [queries, new_keys[:, None], new_values[:, None], offset_row], axis=1
    )[child_of]
    asked = lax.all_to_all(request, "row", split_axis=0, concat_axis=0, tiled=True)
    wanted = asked[:, group_size + 2, 0].astype(jnp.int32)
    answer = attend(
        asked[:, :group_size],
        cache_keys[wanted],
        cache_values[wanted],
        asked[:, group_size],
        asked[:, group_size + 1],
        lengths[wanted],
    )
    attended = lax.all_to_all(answer, "row", split_axis=0, concat_axis=0, tiled=True)[slot_index]
    stream = residual.astype(jnp.float32) + attended.astype(jnp.float32)
    if panel_width % LANES or vocab_weight.shape[2] % 16:
        return project_whole(stream, norm_gain, vocab_weight)
    square_sums = jnp.broadcast_to(
        jnp.sum(stream * stream, axis=(1, 2))[:, None], (beam_count, LANES)
    )
    gained = (stream * norm_gain.astype(jnp.float32)[None]).astype(jnp.bfloat16)
    flat_rows = gained.reshape(beam_count, group_size * panel_width)
    return project(flat_rows, square_sums, jnp.swapaxes(vocab_weight, 1, 2))


def solution(mesh):
    placed = (
        P("row", None, "col"),
        P("row", "col"),
        P("row", "col"),
        P("row", None, "col"),
        P("row", None, "col"),
        P("row"),
        P("row"),
        P("row", None, "col"),
        P(None, "col"),
        P(None, "col", "row"),
    )
    return jax.shard_map(
        body, mesh=mesh, in_specs=placed, out_specs=P("col", "row"), check_vma=False
    )
```

```python
import functools

import jax
import jax.numpy as jnp
from jax import lax
from jax.experimental import pallas as pl
from jax.experimental.pallas import tpu as pltpu
from jax.sharding import PartitionSpec as P

HEAD_DIM = 128
D = 16384
MESH = pl.DeviceIdType.MESH
LANES = 128
CHUNK = 512
PIECE = 256
SLOTS = 10


def from_partner(value, axis, distance):
    mask = 2**distance
    pairs = [(source, source ^ mask) for source in range(lax.axis_size(axis))]
    return lax.ppermute(value, axis, pairs)


def count_before(sources):
    entries = sources.shape[-1]
    earlier = jnp.arange(entries)[:, None] > jnp.arange(entries)[None, :]
    matching = sources[..., :, None] == sources[..., None, :]
    return jnp.sum(matching & earlier, axis=-1)


def attend(queries_in, key_cache, value_cache, key_new, value_new, live_rows):
    leading = queries_in.shape[:-2]
    group_size = queries_in.shape[-2]
    panel_width = queries_in.shape[-1]
    head_part = min(panel_width, HEAD_DIM)
    heads_here = panel_width // head_part
    context = key_cache.shape[-2]
    query_heads = queries_in.reshape(leading + (group_size, heads_here, head_part))
    key_heads = key_cache.reshape(leading + (context, heads_here, head_part))
    value_heads = value_cache.reshape(leading + (context, heads_here, head_part))
    fresh_key = key_new.reshape(leading + (heads_here, head_part))
    fresh_value = value_new.reshape(leading + (1, heads_here, head_part)).astype(jnp.float32)
    cached = jnp.einsum(
        "...jhe,...the->...jht", query_heads, key_heads, preferred_element_type=jnp.float32
    )
    own_score = jnp.einsum(
        "...jhe,...he->...jh", query_heads, fresh_key, preferred_element_type=jnp.float32
    )
    partners = (HEAD_DIM // head_part).bit_length() - 1
    for bit_index in range(partners):
        other_cached, other_own = from_partner((cached, own_score), "col", bit_index)
        cached = cached + other_cached
        own_score = own_score + other_own
    scale_factor = HEAD_DIM ** (-0.5)
    cached = cached * scale_factor
    own_score = own_score * scale_factor
    positions = lax.broadcasted_iota(jnp.int32, cached.shape, cached.ndim - 1)
    visible = positions < live_rows.reshape(leading + (1, 1, 1))
    peak_score = jnp.maximum(jnp.max(jnp.where(visible, cached, -jnp.inf), axis=-1), own_score)
    weight = jnp.where(visible, jnp.exp(cached - peak_score[..., None]), jnp.float32(0.0))
    weight_own = jnp.exp(own_score - peak_score)
    weight_sum = jnp.sum(weight, axis=-1) + weight_own
    rounded = weight.astype(jnp.bfloat16)
    rounded_own = lax.optimization_barrier(weight_own.astype(jnp.bfloat16)).astype(jnp.float32)
    summed = jnp.einsum(
        "...jht,...the->...jhe", rounded, value_heads, preferred_element_type=jnp.float32
    )
    own_part = rounded_own[..., None] * fresh_value
    result = (summed + own_part) / weight_sum[..., None]
    return result.reshape(leading + (group_size, panel_width)).astype(jnp.bfloat16)


def exchange_kernel(n_row, send_ref, out_ref, landing, send_sem, recv_sem):
    row, col = lax.axis_index("row"), lax.axis_index("col")
    barrier = pltpu.get_barrier_semaphore()
    for k in range(1, n_row):
        pl.semaphore_signal(
            barrier, inc=1, device_id=(lax.rem(row + k, n_row), col), device_id_type=MESH
        )
    pl.semaphore_wait(barrier, n_row - 1)
    copies = []
    for k in range(1, n_row):
        to_row = lax.rem(row + k, n_row)
        copy = pltpu.make_async_remote_copy(
            src_ref=send_ref.at[to_row],
            dst_ref=landing.at[row],
            send_sem=send_sem.at[k - 1],
            recv_sem=recv_sem.at[k - 1],
            device_id=(to_row, col),
            device_id_type=MESH,
        )
        copy.start()
        copies.append(copy)
    landing[row] = send_ref[row]
    for copy in copies:
        copy.wait_recv()
    out_ref[...] = landing[...]
    for copy in copies:
        copy.wait_send()


def exchange(value, collective_id):
    n_row, count, width = value.shape
    if width % LANES or count % 16:
        return lax.all_to_all(value, "row", split_axis=0, concat_axis=0, tiled=True)
    vmem = pl.BlockSpec(memory_space=pltpu.VMEM)
    return pl.pallas_call(
        functools.partial(exchange_kernel, n_row),
        out_shape=jax.ShapeDtypeStruct(value.shape, value.dtype),
        in_specs=[vmem],
        out_specs=vmem,
        scratch_shapes=[
            pltpu.VMEM(value.shape, value.dtype),
            pltpu.SemaphoreType.DMA((n_row - 1,)),
            pltpu.SemaphoreType.DMA((n_row - 1,)),
        ],
        compiler_params=pltpu.CompilerParams(collective_id=collective_id, has_side_effects=True),
        cost_estimate=pl.CostEstimate(flops=0, bytes_accessed=4 * value.size, transcendentals=0),
    )(value)


def project_kernel(
    n_row,
    n_col,
    x_ref,
    square_ref,
    weight_ref,
    out_ref,
    rows,
    squares,
    squares_in,
    weights,
    weights_last,
    own,
    outgoing,
    incoming,
    total_out,
    total_in,
    weight_sem,
    last_sem,
    gather_send,
    gather_recv,
    gather_sq_send,
    gather_sq_recv,
    square_send,
    square_recv,
    part_send,
    part_recv,
    total_send,
    total_recv,
):
    row, col = lax.axis_index("row"), lax.axis_index("col")
    beams = x_ref.shape[0]
    groups, vocab, panel = weight_ref.shape
    owned = out_ref.shape[0]
    full = vocab // CHUNK
    last = vocab - full * CHUNK
    last_pad = own.shape[1] - full * CHUNK
    slots = weights.shape[0]
    chips = n_row // 2
    core = lax.rem(row, 2)
    chip = lax.div(row, 2)

    def fetch(chunk, slot):
        return pltpu.make_async_copy(
            weight_ref.at[:, pl.ds(pl.multiple_of(chunk * CHUNK, CHUNK), CHUNK), :],
            weights.at[slot],
            weight_sem.at[slot],
        )

    def fetch_last():
        return pltpu.make_async_copy(
            weight_ref.at[:, pl.ds(full * CHUNK, last), :], weights_last, last_sem.at[0]
        )

    if last:
        fetch_last().start()
    for slot in range(min(slots, full)):
        fetch(slot, slot).start()

    barrier = pltpu.get_barrier_semaphore()
    for k in range(1, n_row):
        pl.semaphore_signal(
            barrier, inc=1, device_id=(lax.rem(row + k, n_row), col), device_id_type=MESH
        )
    for k in range(1, n_col):
        pl.semaphore_signal(
            barrier, inc=1, device_id=(row, lax.rem(col + k, n_col)), device_id_type=MESH
        )
    pl.semaphore_wait(barrier, n_row - 1 + n_col - 1)

    def place(of_row):
        first = of_row * beams
        block = lax.rem(lax.div(first, owned) - col + n_col, n_col)
        return pl.ds(pl.multiple_of(block * owned + lax.rem(first, owned), beams), beams)

    def share(source, target, of_row, to_row, send, recv, index):
        return pltpu.make_async_remote_copy(
            src_ref=source,
            dst_ref=target.at[place(of_row)],
            send_sem=send.at[index],
            recv_sem=recv.at[index],
            device_id=(to_row, col),
            device_id_type=MESH,
        )

    mate = chip * 2 + 1 - core
    started = []
    for k in list(range(1, chips)) + [0]:
        to_row = lax.rem(chip + k, chips) * 2 + core if k else mate
        one = share(x_ref, rows, row, to_row, gather_send, gather_recv, k)
        two = share(square_ref, squares, row, to_row, gather_sq_send, gather_sq_recv, k)
        one.start()
        two.start()
        started += [one, two]
    rows[place(row)] = x_ref[...]
    squares[place(row)] = square_ref[...]
    pad = own.shape[1] - full * CHUNK
    if pad > last:
        edge = own.shape[1] - LANES
        outgoing[:, :, edge:] = jnp.zeros(outgoing.shape[:2] + (LANES,), outgoing.dtype)
        own[:, edge:] = jnp.zeros((owned, LANES), own.dtype)
    forwarded = []
    for k in range(1, chips):
        from_row = lax.rem(chip - k + chips, chips) * 2 + core
        share(rows.at[place(from_row)], rows, row, mate, gather_send, gather_recv, k).wait_recv()
        share(
            squares.at[place(from_row)], squares, row, mate, gather_sq_send, gather_sq_recv, k
        ).wait_recv()
        one = share(
            rows.at[place(from_row)], rows, from_row, mate, gather_send, gather_recv, chips + k
        )
        two = share(
            squares.at[place(from_row)],
            squares,
            from_row,
            mate,
            gather_sq_send,
            gather_sq_recv,
            chips + k,
        )
        one.start()
        two.start()
        forwarded += [one, two]
    for copy in started[-2:]:
        copy.wait_recv()
    for copy in forwarded:
        copy.wait_recv()

    square_copies = []
    for j in range(1, n_col):
        copy = pltpu.make_async_remote_copy(
            src_ref=squares.at[pl.ds(j * owned, owned)],
            dst_ref=squares_in.at[j - 1],
            send_sem=square_send.at[j - 1],
            recv_sem=square_recv.at[j - 1],
            device_id=(row, lax.rem(col + j, n_col)),
            device_id_type=MESH,
        )
        copy.start()
        square_copies.append(copy)

    def part_copy(j, chunk, columns):
        return pltpu.make_async_remote_copy(
            src_ref=outgoing.at[j - 1, :, columns],
            dst_ref=incoming.at[j - 1, :, columns],
            send_sem=part_send.at[chunk, j - 1],
            recv_sem=part_recv.at[chunk, j - 1],
            device_id=(row, lax.rem(col + j, n_col)),
            device_id_type=MESH,
        )

    def columns_of(chunk):
        return pl.ds(pl.multiple_of(chunk * CHUNK, CHUNK), CHUNK)

    last_columns = pl.ds(full * CHUNK, last_pad)

    def product(block, first, width):
        part = jnp.zeros((rows.shape[0], width), jnp.float32)
        for group in range(groups):
            part = part + lax.dot_general(
                rows[:, group * panel : (group + 1) * panel],
                block[group, first : first + width],
                (((1,), (1,)), ((), ())),
                preferred_element_type=jnp.float32,
            )
        return part

    def keep(part, columns):
        own[:, columns] = part[:owned]
        for j in range(1, n_col):
            outgoing[j - 1, :, columns] = part[j * owned : (j + 1) * owned].astype(jnp.bfloat16)

    if last:
        fetch_last().wait()
        for first in range(0, last, PIECE):
            width = min(PIECE, last - first)
            keep(
                product(weights_last, first, width),
                slice(full * CHUNK + first, full * CHUNK + first + width),
            )
        for j in range(1, n_col):
            part_copy(j, full, last_columns).start()

    def multiply(chunk, carry):
        slot = lax.rem(chunk, slots)
        fetch(chunk, slot).wait()
        for first in range(0, CHUNK, PIECE):
            columns = pl.ds(pl.multiple_of(chunk * CHUNK + first, PIECE), PIECE)
            keep(product(weights.at[slot], first, PIECE), columns)
        for j in range(1, n_col):
            part_copy(j, chunk, columns_of(chunk)).start()

        @pl.when(chunk + slots < full)
        def _():
            fetch(chunk + slots, slot).start()

        return carry

    lax.fori_loop(0, full, multiply, 0)

    square_sum = squares[:owned]
    for j in range(1, n_col):
        square_copies[j - 1].wait_recv()
        square_sum = square_sum + squares_in[j - 1]
    scale = lax.rsqrt(square_sum / D + 1e-05)[:, :1]

    def combine(chunk, columns):
        logits = own[:, columns]
        for j in range(1, n_col):
            part_copy(j, chunk, columns).wait_recv()
            logits = logits + incoming[j - 1, :, columns].astype(jnp.float32)
        logits = logits * scale
        own[:, columns] = logits
        return logits

    sums = jnp.zeros((owned, 1), jnp.float32)
    if last:
        logits = combine(full, last_columns)
        sums = sums + jnp.sum(jnp.exp(logits[:, :last]), axis=1, keepdims=True)

    def finish(chunk, sums):
        logits = combine(chunk, columns_of(chunk))
        return sums + jnp.sum(jnp.exp(logits), axis=1, keepdims=True)

    sums = lax.fori_loop(0, full, finish, sums)
    total_out[...] = jnp.broadcast_to(sums, total_out.shape)
    total_copies = []
    for k in range(1, n_row):
        copy = pltpu.make_async_remote_copy(
            src_ref=total_out,
            dst_ref=total_in.at[k - 1],
            send_sem=total_send.at[k - 1],
            recv_sem=total_recv.at[k - 1],
            device_id=(lax.rem(row + k, n_row), col),
            device_id_type=MESH,
        )
        copy.start()
        total_copies.append(copy)
    for copy in started + forwarded + square_copies:
        copy.wait_send()

    def sent(chunk, carry):
        for j in range(1, n_col):
            part_copy(j, chunk, columns_of(chunk)).wait_send()
        return carry

    lax.fori_loop(0, full, sent, 0)
    if last:
        for j in range(1, n_col):
            part_copy(j, full, last_columns).wait_send()
    total = total_out[...]
    for copy in total_copies:
        copy.wait_recv()
    for k in range(1, n_row):
        total = total + total_in[k - 1]
    out_ref[...] = own[:, :vocab] - jnp.log(total)[:, :1]
    for copy in total_copies:
        copy.wait_send()


def project(x, square_sums, weight):
    n_row, n_col = lax.axis_size("row"), lax.axis_size("col")
    beams, depth = x.shape
    groups, vocab, panel = weight.shape
    everyone = beams * n_row
    owned = everyone // n_col
    full = vocab // CHUNK
    last = vocab - full * CHUNK
    wide = full * CHUNK + -(-last // LANES) * LANES
    slots = min(SLOTS, full)
    chips = n_row // 2
    others = n_col - 1
    dma = pltpu.SemaphoreType.DMA
    vmem = pl.BlockSpec(memory_space=pltpu.VMEM)
    return pl.pallas_call(
        functools.partial(project_kernel, n_row, n_col),
        out_shape=jax.ShapeDtypeStruct((owned, vocab), jnp.float32),
        in_specs=[vmem, vmem, pl.BlockSpec(memory_space=pl.ANY)],
        out_specs=vmem,
        scratch_shapes=[
            pltpu.VMEM((everyone, depth), jnp.bfloat16),
            pltpu.VMEM((everyone, LANES), jnp.float32),
            pltpu.VMEM((others, owned, LANES), jnp.float32),
            pltpu.VMEM((slots, groups, CHUNK, panel), jnp.bfloat16),
            pltpu.VMEM((groups, max(last, 16), panel), jnp.bfloat16),
            pltpu.VMEM((owned, wide), jnp.float32),
            pltpu.VMEM((others, owned, wide), jnp.bfloat16),
            pltpu.VMEM((others, owned, wide), jnp.bfloat16),
            pltpu.VMEM((owned, LANES), jnp.float32),
            pltpu.VMEM((n_row - 1, owned, LANES), jnp.float32),
            dma((slots,)),
            dma((1,)),
            dma((2 * chips,)),
            dma((2 * chips,)),
            dma((2 * chips,)),
            dma((2 * chips,)),
            dma((others,)),
            dma((others,)),
            dma((full + 1, others)),
            dma((full + 1, others)),
            dma((n_row - 1,)),
            dma((n_row - 1,)),
        ],
        compiler_params=pltpu.CompilerParams(
            collective_id=0, has_side_effects=True, vmem_limit_bytes=56 * 2**20
        ),
        cost_estimate=pl.CostEstimate(
            flops=2 * everyone * depth * vocab,
            bytes_accessed=2 * depth * vocab,
            transcendentals=owned * vocab,
        ),
    )(x, square_sums, weight)


def project_whole(stream, norm_gain, vocab_weight):
    group_size, panel_width = norm_gain.shape
    square_sums = lax.psum(jnp.sum(stream * stream, axis=(1, 2)), "col")
    scaling = lax.rsqrt(square_sums / D + 1e-05)
    normed = (stream * norm_gain.astype(jnp.float32)[None] * scaling[:, None, None]).astype(
        jnp.bfloat16
    )
    gathered = lax.all_gather(normed, "row", axis=0, tiled=True)
    flat_rows = gathered.reshape(gathered.shape[0], group_size * panel_width)
    flat_weight = vocab_weight.reshape(group_size * panel_width, vocab_weight.shape[2])
    partial = jnp.dot(flat_rows, flat_weight, preferred_element_type=jnp.float32)
    logits = lax.psum_scatter(
        partial.astype(jnp.bfloat16), "col", scatter_dimension=0, tiled=True
    ).astype(jnp.float32)
    totals = lax.psum(jnp.sum(jnp.exp(logits), axis=1), "row")
    return logits - jnp.log(totals)[:, None]


def body(
    queries,
    new_keys,
    new_values,
    cache_keys,
    cache_values,
    lengths,
    parents,
    residual,
    norm_gain,
    vocab_weight,
):
    row_count = lax.axis_size("row")
    beam_count = parents.shape[0]
    slot_cap = max(2, (2 * beam_count + row_count - 1) // row_count)
    group_size = queries.shape[1]
    panel_width = queries.shape[2]
    source = parents // beam_count
    slot_index = source * slot_cap + count_before(source)
    slots = row_count * slot_cap
    taken = slot_index[None, :] == jnp.arange(slots, dtype=jnp.int32)[:, None]
    child_of = jnp.sum(jnp.where(taken, jnp.arange(beam_count, dtype=jnp.int32)[None], 0), axis=1)
    offset = (parents % beam_count).astype(jnp.bfloat16)
    offset_row = jnp.broadcast_to(offset[:, None], (beam_count, panel_width))
    small = jnp.stack([new_keys, new_values, offset_row, offset_row], axis=1)
    split = slot_cap * group_size
    request = jnp.concatenate(
        [
            queries[child_of].reshape(row_count, split, panel_width),
            small[child_of].reshape(row_count, 4 * slot_cap, panel_width),
        ],
        axis=1,
    )
    asked = exchange(request, 1)
    asked_queries = asked[:, :split].reshape(slots, group_size, panel_width)
    asked_small = asked[:, split:].reshape(slots, 4, panel_width)
    wanted = asked_small[:, 2, 0].astype(jnp.int32)
    answer = attend(
        asked_queries,
        cache_keys[wanted],
        cache_values[wanted],
        asked_small[:, 0],
        asked_small[:, 1],
        lengths[wanted],
    )
    returned = exchange(answer.reshape(row_count, split, panel_width), 2)
    attended = returned.reshape(slots, group_size, panel_width)[slot_index]
    stream = residual.astype(jnp.float32) + attended.astype(jnp.float32)
    if panel_width % LANES or vocab_weight.shape[2] % 16:
        return project_whole(stream, norm_gain, vocab_weight)
    square_sums = jnp.broadcast_to(
        jnp.sum(stream * stream, axis=(1, 2))[:, None], (beam_count, LANES)
    )
    gained = (stream * norm_gain.astype(jnp.float32)[None]).astype(jnp.bfloat16)
    flat_rows = gained.reshape(beam_count, group_size * panel_width)
    return project(flat_rows, square_sums, jnp.swapaxes(vocab_weight, 1, 2))


def solution(mesh):
    placed = (
        P("row", None, "col"),
        P("row", "col"),
        P("row", "col"),
        P("row", None, "col"),
        P("row", None, "col"),
        P("row"),
        P("row"),
        P("row", None, "col"),
        P(None, "col"),
        P(None, "col", "row"),
    )
    return jax.shard_map(
        body, mesh=mesh, in_specs=placed, out_specs=P("col", "row"), check_vma=False
    )
```
